128 devices in a mesh: tm: 4 (over x_lo, core), row: 32 (over y, z, x_hi).
Axes of the slice: x: 4 (x_hi: 2, x_lo: 2; x = x_hi * 2 + x_lo), y: 4, z: 4, core: 2. Of those that a mesh axis runs over, the one named last changes fastest.
Arguments:
- queries: bfloat16 [8, 64, 56, 5120], P('tm', 'row'), may hold values from -145 to 145
- frame_keys: bfloat16 [8, 64, 56, 5120], P('tm', 'row'), may hold values from -6.5 to 6.5
- frame_values: bfloat16 [8, 64, 56, 5120], P('tm', 'row'), may hold values from -6 to 6
- tile_mask: int32 [8, 64], P('tm', 'row'), may hold values 0 or 1
- memory_keys: bfloat16 [20, 64, 56, 5120], P('tm', 'row'), may hold values from -6.5 to 6.5
- memory_values: bfloat16 [20, 64, 56, 5120], P('tm', 'row'), may hold values from -6 to 6
- store_slot: int32 [20], replicated, may hold values from 0 to 19, as said below
- retrieved: int32 [8, 2], replicated, may hold values from 0 to 19, as said below
- valid_count: int32 [8], replicated, may hold values from 1 to 2
Outputs:
- attended: bfloat16 [8, 64, 56, 5120], P('tm', 'row')
The draws below stay inside these ranges and needn't reach their ends.
Inputs may be any that keep to these rules, and one draw needn't show every extreme that they name: `store_slot`: each store position appears once. `retrieved`: for each time slab of 2 consecutive frames, at most 2 of its 4 list entries (padded ones included) name frames whose store positions lie in one aligned block 5t to 5t+4 (the positions of one owner along tm), and in every slab some such block is named exactly 2 times.
All inputs are finite; a program needn't handle non-finite values. No bound on the sum of `tile_mask` on one device may be relied on, other than what follows from the above.
Results may differ from the reference program's by a relative error of at most 0.0033.
Values may be sent and summed in bfloat16 or wider, within the bound.
No kernel may reach another device: no remote copies, remote signals or barrier semaphores. Data moves between devices by JAX's collectives and lax.ppermute only.
A program may use at most 192 MiB of HBM per device.

```python
import jax
import jax.numpy as jnp
from jax import lax

D = 5120
HEADS = 40
HD = 128
W = 56
CW = 8
MR = 1
FT_DEV = 2
ROWS_DEV = 2
MEM_DEV = 5
MEM_K = 2
CAP = 2
NF = 8
NR = 64
MEM_FRAMES = 20
N_TM = 4
N_ROW = 32


def key_grid(key):
    folded = jax.random.fold_in(key, 31)
    values_now = jnp.clip(jax.random.normal(jax.random.fold_in(folded, 1), (NF, NR, W, D), jnp.float32), -6.0, 6.0)
    jitter = jnp.clip(jax.random.normal(jax.random.fold_in(folded, 2), (NF, NR, W, D), jnp.float32), -6.0, 6.0)
    column_ids = jnp.arange(W)
    tied = values_now + 0.08 * jitter
    paired = (column_ids % 8 == 3)[None, None, :, None]
    return jnp.where(paired, tied, values_now)


def memory_grid(key):
    folded = jax.random.fold_in(key, 32)
    values_now = jnp.clip(jax.random.normal(jax.random.fold_in(folded, 1), (MEM_FRAMES, NR, W, D), jnp.float32), -6.0, 6.0)
    jitter = jnp.clip(jax.random.normal(jax.random.fold_in(folded, 2), (MEM_FRAMES, NR, W, D), jnp.float32), -6.0, 6.0)
    column_ids = jnp.arange(W)
    tied = values_now + 0.08 * jitter
    paired = (column_ids % 8 == 5)[None, None, :, None]
    return jnp.where(paired, tied, values_now)


def shuffle_row(row_key, row_values):
    return jax.random.permutation(row_key, row_values)


def route_tables(key):
    folded = jax.random.fold_in(key, 41)
    slot_table = jax.random.permutation(jax.random.fold_in(folded, 1), MEM_FRAMES).astype(jnp.int32)
    frame_at = jnp.argsort(slot_table, stable=True).astype(jnp.int32)
    entries = FT_DEV * MEM_K
    main_owner = jax.random.randint(jax.random.fold_in(folded, 2), (N_TM,), 0, N_TM)
    others = (main_owner[:, None] + 1 + jnp.arange((N_TM - 1) * CAP)[None, :] // CAP) % N_TM
    others = jax.vmap(shuffle_row)(jax.random.split(jax.random.fold_in(folded, 3), N_TM), others)
    owners = jnp.concatenate([jnp.broadcast_to(main_owner[:, None], (N_TM, CAP)), others[:, :entries - CAP]], 1)
    owners = jax.vmap(shuffle_row)(jax.random.split(jax.random.fold_in(folded, 4), N_TM), owners)
    local_ids = jax.random.randint(jax.random.fold_in(folded, 5), (N_TM, entries), 0, MEM_DEV)
    positions = (owners * MEM_DEV + local_ids).reshape(NF, MEM_K).astype(jnp.int32)
    return (slot_table, frame_at[positions])


def draw_store_slot(key, part):
    return route_tables(key)[0]


def draw_retrieved(key, part):
    return route_tables(key)[1]


def draw_valid_count(key, part):
    key = jax.random.fold_in(key, 5)
    counts = jax.random.randint(key, (NF,), 1, MEM_K + 1).astype(jnp.int32)
    return counts.at[0].set(MEM_K)


def draw_frame_keys(key, part):
    return key_grid(key).astype(jnp.bfloat16)


def draw_memory_keys(key, part):
    return memory_grid(key).astype(jnp.bfloat16)


def draw_queries(key, part):
    key = jax.random.fold_in(key, 7)
    drawn_part = 2.0 * jnp.clip(jax.random.normal(key, (NF, NR, W, D), jnp.float32), -6.0, 6.0)
    lifted = drawn_part
    return lifted.astype(jnp.bfloat16)


def plant(drawn, stream_key, least, top_value):
    shape = drawn.shape
    spot = [jax.random.randint(jax.random.fold_in(stream_key, axis), (), 0, shape[axis]) for axis in range(len(shape))]
    drawn = drawn.at[tuple(spot)].set(least)
    longest = shape.index(max(shape))
    spot[longest] = (spot[longest] + 1) % shape[longest]
    return drawn.at[tuple(spot)].set(top_value)


def steps_of(rng, extent, cuts, smallest, top_value):
    gain, own = 1.0, jax.random.fold_in(rng, 6)
    for dim, shards_of in cuts:
        heights = jnp.exp(jax.random.uniform(jax.random.fold_in(own, dim), (shards_of,), jnp.float32, smallest / len(cuts), top_value / len(cuts)))
        gain = gain * jnp.repeat(heights, extent[dim] // shards_of).reshape([-1 if axis == dim else 1 for axis in range(len(extent))])
    return gain


def gaussian(own_key, shape, width, reach, cuts=(), held_as=jnp.bfloat16):
    result = jax.random.normal(own_key, shape, jnp.float32) * width
    if len(cuts) > 0:
        result = steps_of(own_key, shape, cuts, -0.22, 0.18) * result
    return jnp.clip(result, min=-reach, max=reach).astype(held_as)


def setup_inputs(seed: int = 0) -> dict:
    splits = jax.random.split(jax.random.key(seed), 10)
    return {
        "queries": draw_queries(jax.random.fold_in(splits[9], 71), 0),
        "frame_keys": draw_frame_keys(jax.random.fold_in(splits[9], 71), 0),
        "frame_values": gaussian(splits[2], (NF, NR, W, D), 1.0, 6.0, ((0, 4), (1, 32))),
        "tile_mask": plant((jax.random.randint(splits[3], (NF, NR), 0, 4) < 3).astype(jnp.int32), jax.random.fold_in(splits[3], 1), 0, 1),
        "memory_keys": draw_memory_keys(jax.random.fold_in(splits[9], 71), 0),
        "memory_values": gaussian(splits[5], (MEM_FRAMES, NR, W, D), 1.0, 6.0, ((0, 4), (1, 32))),
        "store_slot": draw_store_slot(jax.random.fold_in(splits[9], 71), 0),
        "retrieved": draw_retrieved(jax.random.fold_in(splits[9], 71), 0),
        "valid_count": draw_valid_count(jax.random.fold_in(splits[9], 71), 0),
    }


def attend(query_rows, key_rows, value_rows, allowed):
    scores = jnp.einsum("qhd,khd->hqk", query_rows.astype(jnp.float32), key_rows.astype(jnp.float32)) * (HD ** -0.5)
    scores = jnp.where(allowed[None], scores, -1e30)
    row_top = jnp.max(scores, axis=-1, keepdims=True)
    raised = jnp.exp(scores - row_top)
    row_total = jnp.sum(raised, axis=-1)
    weights = lax.optimization_barrier(raised.astype(jnp.bfloat16)).astype(jnp.float32)
    summed = jnp.einsum("hqk,khd->qhd", weights, value_rows.astype(jnp.float32))
    return summed / jnp.transpose(row_total)[:, :, None]


def reference(queries, frame_keys, frame_values, tile_mask, memory_keys, memory_values, store_slot, retrieved, valid_count):
    padded_k = jnp.pad(frame_keys, ((1, 1), (1, 1), (0, 0), (0, 0)))
    padded_v = jnp.pad(frame_values, ((1, 1), (1, 1), (0, 0), (0, 0)))
    padded_mask = jnp.pad(tile_mask, 1)
    columns = jnp.arange(W)
    near_cols = jnp.abs(columns[:, None] - columns[None, :]) <= CW
    centre = jnp.arange(9) == 4

    def self_tile(tile_index):
        frame_no = tile_index // NR
        row_no = tile_index % NR
        zero = jnp.zeros((), jnp.int32)
        tile_k = lax.dynamic_slice(padded_k, (frame_no, row_no, zero, zero), (3, 3, W, D)).reshape(9 * W, HEADS, HD)
        tile_v = lax.dynamic_slice(padded_v, (frame_no, row_no, zero, zero), (3, 3, W, D)).reshape(9 * W, HEADS, HD)
        tile_open = (lax.dynamic_slice(padded_mask, (frame_no, row_no), (3, 3)).reshape(9) == 1) | centre
        allowed = (near_cols[:, None, :] & tile_open[None, :, None]).reshape(W, 9 * W)
        tile_q = lax.dynamic_slice(queries, (frame_no, row_no, zero, zero), (1, 1, W, D)).reshape(W, HEADS, HD)
        return attend(tile_q, tile_k, tile_v, allowed).reshape(W, D)

    self_out = lax.map(self_tile, jnp.arange(NF * NR, dtype=jnp.int32)).reshape(NF, NR, W, D)

    span = ROWS_DEV + 2 * MR
    padded_mk = jnp.pad(memory_keys, ((0, 0), (MR, MR), (0, 0), (0, 0)))
    padded_mv = jnp.pad(memory_values, ((0, 0), (MR, MR), (0, 0), (0, 0)))

    def memory_band(tile_index):
        frame_no = tile_index // N_ROW
        band_no = tile_index % N_ROW
        zero = jnp.zeros((), jnp.int32)
        frame_ids = lax.dynamic_index_in_dim(retrieved, frame_no, 0, keepdims=False)
        slot_ids = store_slot[frame_ids].astype(jnp.int32)
        start_row = (band_no * ROWS_DEV).astype(jnp.int32)
        key_parts = [lax.dynamic_slice(padded_mk, (slot_ids[slot_no], start_row, zero, zero), (1, span, W, D)) for slot_no in range(MEM_K)]
        value_parts = [lax.dynamic_slice(padded_mv, (slot_ids[slot_no], start_row, zero, zero), (1, span, W, D)) for slot_no in range(MEM_K)]
        band_k = jnp.concatenate(key_parts, 0).reshape(MEM_K * span * W, HEADS, HD)
        band_v = jnp.concatenate(value_parts, 0).reshape(MEM_K * span * W, HEADS, HD)
        live_count = lax.dynamic_index_in_dim(valid_count, frame_no, 0, keepdims=False)
        open_entry = jnp.arange(MEM_K) < live_count
        key_row = start_row - MR + jnp.arange(span, dtype=jnp.int32)
        query_row = start_row + jnp.arange(ROWS_DEV, dtype=jnp.int32)
        row_ok = (jnp.abs(key_row[None, :] - query_row[:, None]) <= MR) & (key_row >= 0)[None, :] & (key_row < NR)[None, :]
        allowed = row_ok[:, None, None, :, None] & open_entry[None, None, :, None, None]
        allowed = jnp.broadcast_to(allowed, (ROWS_DEV, W, MEM_K, span, W)).reshape(ROWS_DEV * W, MEM_K * span * W)
        band_q = lax.dynamic_slice(queries, (frame_no, start_row, zero, zero), (1, ROWS_DEV, W, D)).reshape(ROWS_DEV * W, HEADS, HD)
        return attend(band_q, band_k, band_v, allowed).reshape(ROWS_DEV, W, D)

    memory_out = lax.map(memory_band, jnp.arange(NF * N_ROW, dtype=jnp.int32)).reshape(NF, NR, W, D)
    return (self_out + memory_out).astype(jnp.bfloat16)
```

```python
import functools
import math

import jax
import jax.numpy as jnp
import numpy as np
from jax import lax
from jax.experimental import pallas as pl
from jax.experimental.pallas import tpu as pltpu
from jax.sharding import PartitionSpec as P

HD = 128
CW = 8
MEM_K = 2
SEG = 64
NEG = -1e30
SCALE = HD ** (-0.5) * math.log2(math.e)
AXES = ("tm", "row")
CHUNKS = 2
VMEM = 56 * 1024 * 1024


def biases(columns):
    key_row = np.repeat(np.arange(2), columns)[:, None]
    key_col = np.tile(np.arange(columns), 2)[:, None]
    query_row = np.repeat(np.arange(4) - 1, SEG)[None]
    query_col = np.tile(np.arange(SEG), 4)[None]
    pad = query_col >= columns
    rows_ok = np.abs(key_row - query_row) <= 1
    cols_ok = np.abs(key_col - query_col) <= CW
    window = np.where(rows_ok & (cols_ok | pad), 0.0, NEG).astype(np.float32)
    memory = np.where(rows_ok, 0.0, NEG).astype(np.float32)
    own = (key_row == query_row).astype(np.float32)
    return window, memory, own


def fill_bias(table, sf, slot, window_ref, own_ref, bias_ref):
    closed0 = jnp.where(table[40 + slot * 2] == 1, 0.0, NEG)
    closed1 = jnp.where(table[40 + slot * 2 + 1] == 1, 0.0, NEG)
    same = jnp.where(table[sf * 4 + slot] == 2, 1.0, 0.0)
    half = bias_ref.shape[0] // 2
    row = lax.broadcasted_iota(jnp.int32, bias_ref.shape, 0)
    closed = jnp.where(row < half, closed0, closed1)
    bias_ref[...] = window_ref[...] + jnp.where(own_ref[...] * same > 0.5, 0.0, closed)


def for_slots(table, frame_refs, memory_refs, window_ref, memory_ref, own_ref, bias_ref, work):
    sf = pl.program_id(0)
    for slot in range(4):

        @pl.when(table[sf * 4 + slot] > 0)
        def _(slot=slot):
            fill_bias(table, sf, slot, window_ref, own_ref, bias_ref)
            work([refs[slot // 2] for refs in frame_refs], slot % 2, bias_ref, 0)

    for entry in range(MEM_K):
        for place in range(2):

            @pl.when(table[16 + sf * 2 + entry] == place + 1)
            def _(entry=entry, place=place):
                work([refs[place * 2 + entry] for refs in memory_refs], 0, memory_ref, 2)


def scores_of(k_ref, position, q_ref, bias_ref, lanes):
    s = lax.dot_general(
        k_ref[position, :, lanes],
        q_ref[0, :, lanes],
        (((1,), (1,)), ((), ())),
        preferred_element_type=jnp.float32,
    )
    return s * SCALE + bias_ref[...]


def stats_kernel(table, q_ref, ko, ks, mo0, mo1, ms0, ms1, window_ref, memory_ref, own_ref, st_ref, bias_ref):
    heads = st_ref.shape[2]
    for kind in (0, 2):
        st_ref[0, kind] = jnp.full(st_ref.shape[2:], NEG, jnp.float32)
        st_ref[0, kind + 1] = jnp.zeros(st_ref.shape[2:], jnp.float32)

    def work(refs, position, bias, kind):
        def head(h, carry):
            lanes = pl.ds(pl.multiple_of(h * HD, HD), HD)
            s = scores_of(refs[0], position, q_ref, bias, lanes)
            top_old = st_ref[0, kind, pl.ds(h, 1), :]
            top = jnp.maximum(top_old, jnp.max(s, axis=0, keepdims=True))
            part = jnp.sum(jnp.exp2(s - top), axis=0, keepdims=True)
            kept = st_ref[0, kind + 1, pl.ds(h, 1), :] * jnp.exp2(top_old - top)
            st_ref[0, kind, pl.ds(h, 1), :] = top
            st_ref[0, kind + 1, pl.ds(h, 1), :] = kept + part
            return carry

        lax.fori_loop(0, heads, head, 0, unroll=math.gcd(heads, 5))

    for_slots(table, [(ko, ks)], [(mo0, mo1, ms0, ms1)], window_ref, memory_ref, own_ref, bias_ref, work)


def output_kernel(
    table, q_ref, tot_ref, ko, ks, vo, vs, mo0, mo1, ms0, ms1, wo0, wo1, ws0, ws1,
    window_ref, memory_ref, own_ref, o_ref, acc_ref, bias_ref,
):
    heads = tot_ref.shape[2]
    columns = o_ref.shape[2]
    acc_ref[...] = jnp.zeros(acc_ref.shape, jnp.float32)

    def work(refs, position, bias, kind):
        k_ref, v_ref = refs

        def head(h, carry):
            lanes = pl.ds(pl.multiple_of(h * HD, HD), HD)
            s = scores_of(k_ref, position, q_ref, bias, lanes)
            top = tot_ref[0, kind, pl.ds(h, 1), :]
            total = tot_ref[0, kind + 1, pl.ds(h, 1), :]
            weights = jnp.exp2(s - top).astype(jnp.bfloat16)
            part = lax.dot_general(
                v_ref[position, :, lanes],
                weights,
                (((0,), (0,)), ((), ())),
                preferred_element_type=jnp.float32,
            )
            share = jnp.where(total > 0, 1.0 / total, 0.0)
            acc_ref[h] += part * share
            return carry

        lax.fori_loop(0, heads, head, 0, unroll=math.gcd(heads, 5))

    for_slots(
        table, [(ko, ks), (vo, vs)], [(mo0, mo1, ms0, ms1), (wo0, wo1, ws0, ws1)],
        window_ref, memory_ref, own_ref, bias_ref, work,
    )

    def finish(h, carry):
        lanes = pl.ds(pl.multiple_of(h * HD, HD), HD)
        turned = jnp.transpose(acc_ref[h])
        for piece in range(4):
            o_ref[0, piece, :, lanes] = turned[piece * SEG : piece * SEG + columns]
        return carry

    lax.fori_loop(0, heads, finish, 0, unroll=math.gcd(heads, 2))


def kernel_specs(band, width, chunk):
    query = pl.BlockSpec((1, 4 * SEG, width), lambda sf, t: (sf, 0, 0))
    frame = pl.BlockSpec((2, band, width), lambda sf, t: (0, 0, chunk))
    own = [pl.BlockSpec((1, band, width), lambda sf, t, e=e: (t[24 + sf * 2 + e], 0, chunk)) for e in range(MEM_K)]
    sib = [pl.BlockSpec((1, band, width), lambda sf, t, e=e: (t[32 + sf * 2 + e], 0, chunk)) for e in range(MEM_K)]
    mask = pl.BlockSpec((band, 4 * SEG), lambda sf, t: (0, 0))
    return query, frame, own + sib, [mask] * 3


def stats_call(table, q, ko, ks, mo, ms, masks, chunk, heads):
    band, width = ko.shape[1], heads * HD
    query, frame, memory, mask = kernel_specs(band, width, chunk)
    return pl.pallas_call(
        stats_kernel,
        grid_spec=pltpu.PrefetchScalarGridSpec(
            num_scalar_prefetch=1,
            grid=(4,),
            in_specs=[query, frame, frame, *memory, *mask],
            out_specs=pl.BlockSpec((1, 4, heads, 4 * SEG), lambda sf, t: (sf, 0, 0, 0)),
            scratch_shapes=[pltpu.VMEM((band, 4 * SEG), jnp.float32)],
        ),
        out_shape=jax.ShapeDtypeStruct((4, 4, heads, 4 * SEG), jnp.float32),
        compiler_params=pltpu.CompilerParams(vmem_limit_bytes=VMEM),
        cost_estimate=pl.CostEstimate(
            flops=heads * 10 * 2 * band * 4 * SEG * HD,
            bytes_accessed=32 * band * width * 2,
            transcendentals=heads * 10 * band * 4 * SEG,
        ),
        name="stats",
    )(table, q, ko, ks, mo, mo, ms, ms, *masks)


def output_call(table, q, totals, ko, ks, vo, vs, mo, ms, wo, ws, masks, chunk, heads, columns):
    band, width = ko.shape[1], heads * HD
    query, frame, memory, mask = kernel_specs(band, width, chunk)
    return pl.pallas_call(
        output_kernel,
        grid_spec=pltpu.PrefetchScalarGridSpec(
            num_scalar_prefetch=1,
            grid=(4,),
            in_specs=[
                query,
                pl.BlockSpec((1, 4, heads, 4 * SEG), lambda sf, t: (sf, 0, 0, 0)),
                frame, frame, frame, frame, *memory, *memory, *mask,
            ],
            out_specs=pl.BlockSpec((1, 4, columns, width), lambda sf, t: (sf, 0, 0, 0)),
            scratch_shapes=[
                pltpu.VMEM((heads, HD, 4 * SEG), jnp.float32),
                pltpu.VMEM((band, 4 * SEG), jnp.float32),
            ],
        ),
        out_shape=jax.ShapeDtypeStruct((4, 4, columns, width), jnp.float32),
        compiler_params=pltpu.CompilerParams(vmem_limit_bytes=VMEM),
        cost_estimate=pl.CostEstimate(
            flops=heads * 10 * 4 * band * 4 * SEG * HD,
            bytes_accessed=64 * band * width * 2,
            transcendentals=heads * 10 * band * 4 * SEG,
        ),
        name="output",
    )(table, q, totals, ko, ks, vo, vs, mo, mo, ms, ms, wo, wo, ws, ws, *masks)


def merge(parts):
    kinds = []
    for kind in (0, 2):
        tops = [jnp.where(p[:, kind + 1] > 0, p[:, kind], NEG) for p in parts]
        top = functools.reduce(jnp.maximum, tops)
        total = sum(p[:, kind + 1] * jnp.exp2(t - top) for p, t in zip(parts, tops))
        kinds += [top, total]
    return jnp.stack(kinds, 1)


def local(
    queries,
    frame_keys,
    frame_values,
    tile_mask,
    memory_keys,
    memory_values,
    store_slot,
    retrieved,
    valid_count,
):
    frames, rows, columns, width = queries.shape
    slabs, bands = lax.axis_size("tm"), lax.axis_size("row")
    stored = memory_keys.shape[0]
    band = rows * columns
    heads = width // HD // CHUNKS
    part = heads * HD
    slab = lax.axis_index("tm")

    def pairs(slab_of, step):
        return [
            (t * bands + r, slab_of(t) * bands + r + step)
            for t in range(slabs)
            for r in range(bands)
            if 0 <= r + step < bands
        ]

    def core(x):
        return lax.ppermute(x, AXES, pairs(lambda t: t ^ 1, 0))

    def cross(x):
        return lax.ppermute(x, AXES, pairs(lambda t: t ^ 2, 0))

    def down(x):
        return lax.ppermute(x, AXES, pairs(lambda t: t ^ 2, 1))

    def up(x):
        return lax.ppermute(x, AXES, pairs(lambda t: t ^ 2, -1))

    sib = slab ^ 1
    query_frames = jnp.concatenate([slab * frames + jnp.arange(frames), (slab ^ 2) * frames + jnp.arange(frames)])
    key_frames = jnp.concatenate([slab * frames + jnp.arange(frames), sib * frames + jnp.arange(frames)])
    gap = jnp.abs(query_frames[:, None] - key_frames[None, :])
    seen = jnp.where(gap == 0, 2, jnp.where(gap == 1, 1, 0))
    ids = jnp.arange(store_slot.shape[0], dtype=jnp.int32)
    position = jnp.sum(jnp.where(retrieved[:, :, None] == ids, store_slot, 0), axis=-1)
    live = jnp.arange(MEM_K)[None, :] < valid_count[:, None]
    wanted = query_frames[:, None] == jnp.arange(retrieved.shape[0])[None, :]
    place = jnp.sum(jnp.where(wanted[:, :, None], position[None], 0), axis=1)
    alive = jnp.sum(jnp.where(wanted[:, :, None], live[None].astype(jnp.int32), 0), axis=1) > 0
    owner, spot = place // stored, place % stored
    source = jnp.where(alive & (owner == slab), 1, jnp.where(alive & (owner == sib), 2, 0))
    spot_own = jnp.where(source == 1, spot, 0)
    spot_sib = jnp.where(source == 2, spot, 0)
    open_tiles = jnp.concatenate([tile_mask, core(tile_mask)], 0)
    table = jnp.concatenate(
        [v.reshape(-1).astype(jnp.int32) for v in (seen, source, spot_own, spot_sib, open_tiles)]
    )

    ko, vo = frame_keys.reshape(frames, band, width), frame_values.reshape(frames, band, width)
    mo, wo = memory_keys.reshape(stored, band, width), memory_values.reshape(stored, band, width)
    ks, ms = core(ko), core(mo)
    vs, ws = core(vo), core(wo)
    masks = [jnp.asarray(m) for m in biases(columns)]

    asked = []
    for chunk in range(CHUNKS):
        mine = queries[..., chunk * part : (chunk + 1) * part]
        if chunk % 2 == 0:
            theirs = cross(mine)
            both = jnp.concatenate([mine, theirs], 0)
            above, below = down(both[:, 1]), up(both[:, 0])
            above = jnp.concatenate([above[frames:], above[:frames]], 0)
            below = jnp.concatenate([below[frames:], below[:frames]], 0)
        else:
            above, below = down(mine[:, 1]), up(mine[:, 0])
            moved = cross(jnp.concatenate([mine, above[:, None], below[:, None]], 1))
            both = jnp.concatenate([mine, moved[:, :2]], 0)
            above = jnp.concatenate([moved[:, 2], above], 0)
            below = jnp.concatenate([moved[:, 3], below], 0)
        q = jnp.stack([above, both[:, 0], both[:, 1], below], 1)
        q = jnp.pad(q, ((0, 0), (0, 0), (0, SEG - columns), (0, 0)))
        asked.append(q.reshape(2 * frames, 4 * SEG, part))

    stats = [stats_call(table, asked[c], ko, ks, mo, ms, masks, c, heads) for c in range(CHUNKS)]

    totals = []
    for st in stats:
        from_below, from_above = up(st[..., :SEG]), down(st[..., 3 * SEG :])
        edge = jnp.concatenate([from_above, from_below], -1)
        own = st[..., SEG : 3 * SEG]
        joined = cross(merge([own[frames:], edge[:frames]]))
        total = merge([own[:frames], edge[frames:], joined])
        both = jnp.concatenate([total, cross(total)], 0)
        above, below = down(both[..., SEG:]), up(both[..., :SEG])
        above = jnp.concatenate([above[frames:], above[:frames]], 0)
        below = jnp.concatenate([below[frames:], below[:frames]], 0)
        totals.append(jnp.concatenate([above, both, below], -1))

    results = []
    for c in range(CHUNKS):
        o = output_call(table, asked[c], totals[c], ko, ks, vo, vs, mo, ms, wo, ws, masks, c, heads, columns)
        above, own, below = o[:, 0], o[:, 1:3], o[:, 3]
        sent = jnp.bfloat16
        if c % 2 == 0:
            from_below, from_above = up(above.astype(sent)), down(below.astype(sent))
            edge = jnp.stack([from_above, from_below], 1).astype(jnp.float32)
            joined = cross((own[frames:] + edge[:frames]).astype(sent))
            results.append((own[:frames] + edge[frames:] + joined.astype(jnp.float32)).astype(jnp.bfloat16))
        else:
            moved = cross(
                jnp.concatenate([above[:frames, None], own[frames:], below[:frames, None]], 1).astype(sent)
            )
            from_below = up((above[frames:] + moved[:, 0].astype(jnp.float32)).astype(sent))
            from_above = down((below[frames:] + moved[:, 3].astype(jnp.float32)).astype(sent))
            edge = jnp.stack([from_above, from_below], 1).astype(jnp.float32)
            results.append((own[:frames] + edge + moved[:, 1:3].astype(jnp.float32)).astype(jnp.bfloat16))
    return jnp.concatenate(results, -1)


def solution(mesh):
    in_specs = (
        P("tm", "row", None, None),
        P("tm", "row", None, None),
        P("tm", "row", None, None),
        P("tm", "row"),
        P("tm", "row", None, None),
        P("tm", "row", None, None),
        P(),
        P(),
        P(),
    )
    out_specs = P("tm", "row", None, None)
    return jax.shard_map(local, mesh=mesh, in_specs=in_specs, out_specs=out_specs, check_vma=False)
```

```python
import functools
import math

import jax
import jax.numpy as jnp
import numpy as np
from jax import lax
from jax.experimental import pallas as pl
from jax.experimental.pallas import tpu as pltpu
from jax.sharding import PartitionSpec as P

HD = 128
CW = 8
MEM_K = 2
SEG = 64
OWN = 2 * SEG
TILE = 4 * SEG
NEG = -1e30
SCALE = HD ** (-0.5) * math.log2(math.e)
AXES = ("tm", "row")
VMEM = 56 * 1024 * 1024


def masks_of(columns):
    key_row = np.repeat(np.arange(2), columns)[:, None]
    key_col = np.tile(np.arange(columns), 2)[:, None]
    query_row = np.repeat(np.array([0, 1, -1, 2]), SEG)[None]
    query_col = np.tile(np.arange(SEG), 4)[None]
    rows_ok = np.abs(key_row - query_row) <= 1
    cols_ok = (np.abs(key_col - query_col) <= CW) | (query_col >= columns)
    window = np.where(rows_ok & cols_ok, 0.0, NEG).astype(np.float32)
    memory = np.where(rows_ok & (query_col >= 0), 0.0, NEG).astype(np.float32)
    own = np.where(key_row == query_row, 1.0, 0.0) + np.zeros_like(window)
    return [jnp.asarray(m, jnp.float32) for m in (window, memory, own)]


def fill_bias(table, sf, slot, window_ref, own_ref, bias_ref):
    closed = [jnp.where(table[40 + slot * 2 + row] == 1, 0.0, NEG) for row in range(2)]
    same = jnp.where(table[sf * 4 + slot] == 2, 1.0, 0.0)
    row = lax.broadcasted_iota(jnp.int32, bias_ref.shape, 0)
    shut = jnp.where(row < bias_ref.shape[0] // 2, closed[0], closed[1])
    bias_ref[...] = window_ref[...] + jnp.where(own_ref[...] * same > 0.5, 0.0, shut)


def for_slots(table, frame_refs, memory_refs, masks, bias_ref, work):
    window_ref, memory_ref, own_ref = masks
    sf = pl.program_id(0)
    for slot in range(4):

        @pl.when(table[sf * 4 + slot] > 0)
        def _(slot=slot):
            fill_bias(table, sf, slot, window_ref, own_ref, bias_ref)
            work([refs[slot // 2] for refs in frame_refs], slot % 2, bias_ref, 0)

    for entry in range(MEM_K):
        for place in range(2):

            @pl.when(table[16 + sf * 2 + entry] == place + 1)
            def _(entry=entry, place=place):
                work([refs[place * 2 + entry] for refs in memory_refs], 0, memory_ref, 1)


def scores_of(k_ref, position, q_ref, mask, h):
    lanes = slice(h * HD, (h + 1) * HD)
    s = lax.dot_general(
        k_ref[position, :, lanes],
        q_ref[0, :, lanes],
        (((1,), (1,)), ((), ())),
        preferred_element_type=jnp.float32,
    )
    return s * SCALE + mask[...]


def stats_kernel(table, q_ref, ko, ks, mo0, mo1, ms0, ms1, m0, m1, m2, *rest):
    st_ref, bias_ref = rest[-2:]
    heads = st_ref.shape[1] // 4
    for kind in range(2):
        st_ref[0, 2 * kind * heads : (2 * kind + 1) * heads] = jnp.full((heads, TILE), NEG, jnp.float32)
        st_ref[0, (2 * kind + 1) * heads : (2 * kind + 2) * heads] = jnp.zeros((heads, TILE), jnp.float32)

    def work(refs, position, mask, kind):
        joined = []
        for h in range(heads):
            top_at, sum_at = 2 * kind * heads + h, (2 * kind + 1) * heads + h
            s = scores_of(refs[0], position, q_ref, mask, h)
            old = st_ref[0, top_at : top_at + 1, :]
            top = jnp.maximum(old, jnp.max(s, axis=0, keepdims=True))
            part = jnp.sum(jnp.exp2(s - top), axis=0, keepdims=True)
            kept = st_ref[0, sum_at : sum_at + 1, :] * jnp.exp2(old - top)
            joined.append((top_at, top, sum_at, kept + part))
        for top_at, top, sum_at, total in joined:
            st_ref[0, top_at : top_at + 1, :] = top
            st_ref[0, sum_at : sum_at + 1, :] = total

    for_slots(table, [(ko, ks)], [(mo0, mo1, ms0, ms1)], (m0, m1, m2), bias_ref, work)


def output_kernel(
    table, q_ref, t_ref, ko, ks, vo, vs, mo0, mo1, ms0, ms1, wo0, wo1, ws0, ws1, m0, m1, m2,
    *rest,
):
    own_ref, rim_ref, acc_ref, bias_ref = rest[-4:]
    heads = t_ref.shape[1] // 4
    columns = own_ref.shape[2]
    acc_ref[...] = jnp.zeros(acc_ref.shape, jnp.float32)

    def work(refs, position, mask, kind):
        k_ref, v_ref = refs
        sums = []
        for h in range(heads):
            top_at = 2 * kind * heads + h
            s = scores_of(k_ref, position, q_ref, mask, h)
            weights = jnp.exp2(s - t_ref[0, top_at : top_at + 1, :]).astype(jnp.bfloat16)
            part = lax.dot_general(
                weights,
                v_ref[position, :, h * HD : (h + 1) * HD],
                (((0,), (0,)), ((), ())),
                preferred_element_type=jnp.float32,
            )
            acc_ref[kind, h] += part

    for_slots(
        table, [(ko, ks), (vo, vs)], [(mo0, mo1, ms0, ms1), (wo0, wo1, ws0, ws1)], (m0, m1, m2), bias_ref, work
    )
    rows = t_ref.shape[1]
    turned = jnp.concatenate([t_ref[0], jnp.zeros((-rows % 128, TILE), jnp.float32)], 0).T
    for h in range(heads):
        o = (
            acc_ref[0, h] * turned[:, heads + h : heads + h + 1]
            + acc_ref[1, h] * turned[:, 3 * heads + h : 3 * heads + h + 1]
        )
        for piece in range(4):
            ref = (own_ref, rim_ref)[piece // 2]
            ref[0, piece % 2, :, h * HD : (h + 1) * HD] = o[piece * SEG : piece * SEG + columns].astype(ref.dtype)


def specs(band, width, chunk):
    frame = pl.BlockSpec((2, band, width), lambda sf, t: (0, 0, chunk))
    own = [pl.BlockSpec((1, band, width), lambda sf, t, e=e: (t[24 + sf * 2 + e], 0, chunk)) for e in range(MEM_K)]
    sib = [pl.BlockSpec((1, band, width), lambda sf, t, e=e: (t[32 + sf * 2 + e], 0, chunk)) for e in range(MEM_K)]
    mask = pl.BlockSpec((band, TILE), lambda sf, t: (0, 0))
    query = pl.BlockSpec((1, TILE, width), lambda sf, t: (sf, 0, 0))
    stat = pl.BlockSpec((1, 4 * width // HD, TILE), lambda sf, t: (sf, 0, 0))
    return frame, own + sib, [mask] * 3, query, stat


def stats_call(table, q, keys, masks, chunk, after):
    ko, ks, mo, ms = keys
    band, width = ko.shape[1], q.shape[-1]
    heads = width // HD
    frame, memory, mask, query, stat = specs(band, width, chunk)
    return pl.pallas_call(
        stats_kernel,
        grid_spec=pltpu.PrefetchScalarGridSpec(
            num_scalar_prefetch=1,
            grid=(q.shape[0],),
            in_specs=[query, frame, frame, *memory, *mask, *[pl.BlockSpec(memory_space=pl.ANY)] * len(after)],
            out_specs=stat,
            scratch_shapes=[pltpu.VMEM((band, TILE), jnp.float32)],
        ),
        out_shape=jax.ShapeDtypeStruct((q.shape[0], 4 * heads, TILE), jnp.float32),
        compiler_params=pltpu.CompilerParams(vmem_limit_bytes=VMEM),
        cost_estimate=pl.CostEstimate(
            flops=heads * 400_000_000, bytes_accessed=heads * 100_000, transcendentals=heads * 10_000
        ),
        name="stats",
    )(table, q, ko, ks, mo, mo, ms, ms, *masks, *after)


def output_call(table, q, totals, keys, values, masks, chunk, columns, rim_type, after):
    ko, ks, mo, ms = keys
    vo, vs, wo, ws = values
    band, width = ko.shape[1], q.shape[-1]
    heads = width // HD
    frame, memory, mask, query, stat = specs(band, width, chunk)
    part = pl.BlockSpec((1, 2, columns, width), lambda sf, t: (sf, 0, 0, 0))
    return pl.pallas_call(
        output_kernel,
        grid_spec=pltpu.PrefetchScalarGridSpec(
            num_scalar_prefetch=1,
            grid=(q.shape[0],),
            in_specs=[
                query, stat, frame, frame, frame, frame, *memory, *memory, *mask,
                *[pl.BlockSpec(memory_space=pl.ANY)] * len(after),
            ],
            out_specs=[part, part],
            scratch_shapes=[
                pltpu.VMEM((2, heads, TILE, HD), jnp.float32),
                pltpu.VMEM((band, TILE), jnp.float32),
            ],
        ),
        out_shape=[jax.ShapeDtypeStruct((q.shape[0], 2, columns, width), d) for d in (jnp.float32, rim_type)],
        compiler_params=pltpu.CompilerParams(vmem_limit_bytes=VMEM),
        cost_estimate=pl.CostEstimate(
            flops=heads * 500_000_000, bytes_accessed=heads * 100_000, transcendentals=heads * 10_000
        ),
        name="output",
    )(table, q, totals, ko, ks, vo, vs, mo, mo, ms, ms, wo, wo, ws, ws, *masks, *after)


def merge(*parts):
    kinds = []
    for kind in (0, 2):
        tops = [jnp.where(p[:, kind + 1] > 0, p[:, kind], NEG) for p in parts]
        top = functools.reduce(jnp.maximum, tops)
        total = sum(p[:, kind + 1] * jnp.exp2(t - top) for p, t in zip(parts, tops))
        kinds += [top, total]
    return jnp.stack(kinds, 1)


def shares(st):
    flip = [jnp.where(st[:, k] > 0, 1.0 / st[:, k], 0.0) for k in (1, 3)]
    return jnp.stack([st[:, 0], flip[0], st[:, 2], flip[1]], 1)


def local(
    queries,
    frame_keys,
    frame_values,
    tile_mask,
    memory_keys,
    memory_values,
    store_slot,
    retrieved,
    valid_count,
):
    frames, rows, columns, width = queries.shape
    slabs, bands = lax.axis_size("tm"), lax.axis_size("row")
    stored = memory_keys.shape[0]
    band = rows * columns
    heads = width // HD // 2
    part = heads * HD
    slab = lax.axis_index("tm")
    odd = lax.axis_index("row") % 2

    def pairs(slab_of, band_of):
        return [
            (t * bands + r, slab_of(t) * bands + band_of(r))
            for t in range(slabs)
            for r in range(bands)
            if 0 <= band_of(r) < bands
        ]

    def core(x):
        return lax.ppermute(x, AXES, pairs(lambda t: t ^ 1, lambda r: r))

    def cross(x):
        return lax.ppermute(x, AXES, pairs(lambda t: t ^ 2, lambda r: r))

    def near(x):
        return lax.ppermute(x, AXES, pairs(lambda t: t ^ 2, lambda r: r ^ 1))

    def far(x):
        return lax.ppermute(x, AXES, pairs(lambda t: t ^ 2, lambda r: ((r + 1) ^ 1) - 1))

    def pick(which, x, y):
        return jnp.where(which == 0, x, y)

    sib = slab ^ 1
    query_frames = jnp.concatenate([slab * frames + jnp.arange(frames), (slab ^ 2) * frames + jnp.arange(frames)])
    key_frames = jnp.concatenate([slab * frames + jnp.arange(frames), sib * frames + jnp.arange(frames)])
    gap = jnp.abs(query_frames[:, None] - key_frames[None, :])
    seen = jnp.where(gap == 0, 2, jnp.where(gap == 1, 1, 0))
    ids = jnp.arange(store_slot.shape[0], dtype=jnp.int32)
    position = jnp.sum(jnp.where(retrieved[:, :, None] == ids, store_slot, 0), axis=-1)
    live = jnp.arange(MEM_K)[None, :] < valid_count[:, None]
    wanted = query_frames[:, None] == jnp.arange(retrieved.shape[0])[None, :]
    place = jnp.sum(jnp.where(wanted[:, :, None], position[None], 0), axis=1)
    alive = jnp.sum(jnp.where(wanted[:, :, None], live[None].astype(jnp.int32), 0), axis=1) > 0
    owner, spot = place // stored, place % stored
    source = jnp.where(alive & (owner == slab), 1, jnp.where(alive & (owner == sib), 2, 0))
    spot_own = jnp.where(source == 1, spot, 0)
    spot_sib = jnp.where(source == 2, spot, 0)
    sib_tiles = core(tile_mask)
    open_tiles = jnp.concatenate([tile_mask, sib_tiles], 0)
    table = jnp.concatenate(
        [v.reshape(-1).astype(jnp.int32) for v in (seen, source, spot_own, spot_sib, open_tiles)]
    )

    ko, vo = frame_keys.reshape(frames, band, width), frame_values.reshape(frames, band, width)
    mo, wo = memory_keys.reshape(stored, band, width), memory_values.reshape(stored, band, width)
    ks, ms = core(ko), core(mo)
    vs, ws = core(vo), core(wo)
    keys, values = (ko, ks, mo, ms), (vo, vs, wo, ws)

    def nothing(*arrays):
        firsts = [x[(0,) * x.ndim].astype(jnp.float32) for x in arrays]
        return functools.reduce(jnp.add, [(f > 3e38).astype(jnp.int32) for f in firsts])
    masks = masks_of(columns)

    def rows_out(to_above, to_below, odd=odd):
        return pick(odd, to_below, to_above), pick(odd, to_above, to_below)

    def rows_in(by_near, by_far, odd=odd):
        return pick(odd, by_far, by_near), pick(odd, by_near, by_far)

    def swap_rows(to_above, to_below):
        a, b = rows_out(to_above, to_below)
        return rows_in(near(a), far(b))

    def turn(x):
        return jnp.concatenate([x[frames:], x[:frames]], 0)

    def tile_of(own, above, below):
        x = jnp.concatenate([own, above[:, None], below[:, None]], 1)
        x = jnp.pad(x, ((0, 0), (0, 0), (0, SEG - columns), (0, 0)))
        return x.reshape(2 * frames, TILE, part)

    def chips_joined(st):
        other = turn(cross(st.reshape(2 * frames, 4 * heads, TILE))).reshape(st.shape)
        return merge(st, other)

    def bands_joined(st):
        a, b, u, d = (st[..., i * SEG : (i + 1) * SEG] for i in range(4))
        flat = (2 * frames, 4 * heads, OWN)
        above, below = swap_rows(
            jnp.concatenate([u, a], -1).reshape(flat), jnp.concatenate([b, d], -1).reshape(flat)
        )
        above, below = turn(above).reshape(*st.shape[:3], OWN), turn(below).reshape(*st.shape[:3], OWN)
        other = jnp.concatenate([above[..., SEG:], below[..., :SEG], above[..., :SEG], below[..., SEG:]], -1)
        return merge(st, other)

    first, second = queries[..., :part], queries[..., part:]
    theirs = cross(first)
    by_near, by_far = (f(x) for f, x in zip((near, far), rows_out(second[:, 0], second[:, 1], odd + nothing(sib_tiles))))
    ordered = odd + nothing(ks, ms)
    both = jnp.concatenate([first, theirs], 0)
    near0, far0 = rows_out(both[:, 0], both[:, 1], ordered)
    above1, below1 = rows_in(by_near, by_far, ordered)
    moved = cross(jnp.concatenate([second, above1[:, None], below1[:, None]], 1))
    above, below = rows_in(near(near0), far(far0))
    asked = [tile_of(both, turn(above), turn(below))]
    stats = [stats_call(table, asked[0], keys, masks, 0, (moved,))]
    above1, below1 = rows_in(by_near, by_far, odd + nothing(stats[0]))
    asked.append(
        tile_of(
            jnp.concatenate([second, moved[:, :2]], 0),
            jnp.concatenate([moved[:, 2], above1], 0),
            jnp.concatenate([moved[:, 3], below1], 0),
        )
    )
    first = chips_joined(stats[0].reshape(2 * frames, 4, heads, TILE))
    stats.append(stats_call(table, asked[1], keys, masks, 1, (first,)))
    second = bands_joined(stats[1].reshape(2 * frames, 4, heads, TILE))

    sent, full = jnp.bfloat16, jnp.float32
    def by_bands_first(own, rim):
        above, below = swap_rows(rim[:, 0].astype(sent), rim[:, 1].astype(sent))
        edge = turn(jnp.stack([above, below], 1)).astype(full)
        joined = cross((own[frames:] + edge[frames:]).astype(sent))
        return (own[:frames] + edge[:frames] + joined.astype(full)).astype(jnp.bfloat16)

    def by_chips_first(own, rim):
        moved = cross(jnp.concatenate([own[frames:], rim[:frames]], 1).astype(sent))
        ready = (rim[frames:] + moved[:, 2:].astype(full)).astype(sent)
        above, below = swap_rows(ready[:, 0], ready[:, 1])
        edge = jnp.stack([above, below], 1).astype(full)
        return (own[:frames] + edge + moved[:, :2].astype(full)).astype(jnp.bfloat16)

    totals = [shares(bands_joined(first)), shares(chips_joined(second))]
    results = []
    before = ()
    for c in range(2):
        flat = totals[c].reshape(2 * frames, 4 * heads, TILE)
        own, rim = output_call(table, asked[c], flat, keys, values, masks, c, columns, full, before)
        before = (own,)
        half = part // 2
        results.append(by_bands_first(own[..., :half], rim[..., :half]))
        results.append(by_chips_first(own[..., half:], rim[..., half:]))
    return jnp.concatenate(results, -1)


def solution(mesh):
    in_specs = (
        P("tm", "row", None, None),
        P("tm", "row", None, None),
        P("tm", "row", None, None),
        P("tm", "row"),
        P("tm", "row", None, None),
        P("tm", "row", None, None),
        P(),
        P(),
        P(),
    )
    out_specs = P("tm", "row", None, None)
    return jax.shard_map(local, mesh=mesh, in_specs=in_specs, out_specs=out_specs, check_vma=False)
```
